32 devices in a mesh: row: 8 (over z, y), col: 4 (over x, core).
Axes of the slice: x: 2, y: 2, z: 4, core: 2. Of those that a mesh axis runs over, the one named last changes fastest.
Arguments:
- fit_tiles: bfloat16 [16, 24, 128, 128], P('row', 'col'), may hold values from -6 to 6
- aux_list: int32 [16, 24], P('row', 'col'), may hold values from 0 to 11, as said below
- aux_count: int32 [16, 4], P('row', 'col'), may hold values from 1 to 6, as said below
- metric: bfloat16 [48, 128, 128], P('col', 'row'), may hold values from -0.5 to 0.5
Outputs:
- exchange: float32 [2048, 2048], P('col', 'row')
The draws below stay inside these ranges and needn't reach their ends.
Inputs may be any that keep to these rules, and one draw needn't show every extreme that they name: `aux_list`: within one atom block and one col shard, the first 6 slots name distinct auxiliary blocks. `aux_count`: counts follow a density per atom block; the largest is reached in every draw.
All inputs are finite; a program needn't handle non-finite values.
Results may differ from the reference program's by a relative error of at most 0.0015.
Values may be sent and summed in bfloat16 or wider, within the bound.
A program may use at most 64 MiB of HBM per device.

```python
import jax
import jax.numpy as jnp
from jax import lax

BS = 128
AUXB = 128
QB = 12
QS = 6
NS = 16
NQ = 48
NF = 2048
N_COL = 4


def draw_aux_list(key, part):
    scores = jax.random.randint(key, (NS, N_COL, QB), 0, 1 << 20) * QB + jnp.arange(QB, dtype=jnp.int32)
    order = jnp.argsort(scores, axis=-1, stable=True).astype(jnp.int32)
    return order[:, :, :QS].reshape(NS, N_COL * QS)


def draw_aux_count(key, part):
    first = jax.random.fold_in(key, 11)
    second = jax.random.fold_in(key, 12)
    density = jax.random.randint(first, (NS, 1), 1, QS + 1)
    jitter = jax.random.randint(second, (NS, N_COL), 0, 2)
    counts = jnp.clip(density - jitter, 1, QS)
    corner = (jnp.arange(NS)[:, None] == 0) & (jnp.arange(N_COL)[None, :] == 0)
    return jnp.where(corner, QS, counts).astype(jnp.int32)


def block_levels(stream_key, shape, split, low, high):
    def one(position, parts):
        steps = jax.random.uniform(jax.random.fold_in(jax.random.fold_in(stream_key, 6), position), (parts,), jnp.float32, low / len(split), high / len(split))
        return jnp.repeat(jnp.exp(steps), shape[position] // parts).reshape((-1,) + (1,) * (len(shape) - position - 1))

    gain = one(*split[0])
    for cut in split[1:]:
        gain = gain * one(*cut)
    return gain


def noise(stream_key, extent, scale, reach, cuts=(), kind=jnp.bfloat16):
    drawn = jax.random.normal(stream_key, extent, jnp.float32) * scale
    if len(cuts) > 0:
        drawn = block_levels(stream_key, extent, cuts, -0.22, 0.18) * drawn
    return jnp.clip(drawn, min=-reach, max=reach).astype(kind)


def setup_inputs(seed: int = 0) -> dict:
    seeds = jax.random.split(jax.random.key(seed), 5)
    return {
        "fit_tiles": noise(seeds[0], (NS, N_COL * QS, BS, AUXB), 1.0, 6.0, ((0, 8), (1, 4))),
        "aux_list": draw_aux_list(jax.random.fold_in(seeds[4], 71), 0),
        "aux_count": draw_aux_count(jax.random.fold_in(seeds[4], 71), 0),
        "metric": noise(seeds[3], (NQ, AUXB, AUXB), AUXB ** -0.5, 0.5, ((0, 4), (1, 8))),
    }


def reference(fit_tiles, aux_list, aux_count, metric):
    slots = jnp.arange(N_COL * QS, dtype=jnp.int32)
    shard = slots // QS
    local = slots % QS
    live = local[None, :] < aux_count[:, shard]
    qid = (shard[None, :] * QB + aux_list).astype(jnp.int32)

    def one_block(items):
        tiles, ids, alive = items
        mats = metric[ids].astype(jnp.float32)
        fitted = jnp.einsum("smk,skn->smn", tiles.astype(jnp.float32), mats).astype(jnp.bfloat16)
        onehot = ((ids[:, None] == jnp.arange(NQ, dtype=jnp.int32)[None, :]) & alive[:, None]).astype(jnp.float32)
        return jnp.einsum("sq,smn->mqn", onehot, fitted.astype(jnp.float32))

    dense = lax.map(one_block, (fit_tiles, qid, live))
    dense = dense.reshape(NF, NQ * AUXB)
    total = jnp.dot(dense, dense.T, precision=lax.Precision.HIGHEST)
    return total * (1.0 / (QS * N_COL * AUXB) ** 0.5)
```

```python
import functools

import jax
import jax.numpy as jnp
from jax import lax
from jax.experimental import pallas as pl
from jax.experimental.pallas import tpu as pltpu
from jax.sharding import PartitionSpec as P

MESH = pl.DeviceIdType.MESH


def kernel(
    n, m, share, fit, metric, lst, cnt, out,
    mbuf, mfull, gat, note, notes, table, turned, wide, part, red,
    met_send, met_recv, fit_send, fit_recv, note_send, note_recv, table_sem, red_send, red_recv,
):
    atoms, slots, rows, aux = fit.shape
    blocks = metric.shape[0]
    half = n // 2
    hops = (half, n - 1 - half)
    row = lax.axis_index("row")
    col = lax.axis_index("col")

    def at_position(p):
        p = lax.rem(p + n, n)
        return jnp.where(p < (n + 1) // 2, 2 * p, 2 * (n - 1 - p) + 1)

    place = jnp.where(lax.rem(row, 2) == 0, row // 2, n - 1 - row // 2)

    def source(way, step):
        return at_position(place - step if way == 0 else place + step)

    def target(way):
        return at_position(place + 1 if way == 0 else place + n - 1)

    barrier = pltpu.get_barrier_semaphore()
    for k in range(1, n):
        pl.semaphore_signal(barrier, inc=1, device_id=(lax.rem(row + k, n), col), device_id_type=MESH)
    for k in range(1, m):
        pl.semaphore_signal(barrier, inc=1, device_id=(row, lax.rem(col + k, m)), device_id_type=MESH)
    note[...] = jnp.zeros_like(note)
    note[0:atoms, 0:slots] = lst[...]
    note[0:atoms, slots : slots + 1] = cnt[...]
    notes[row] = note[...]
    mbuf[row] = metric[...]
    pl.semaphore_wait(barrier, n + m - 2)

    def met_copy(way, step, src, owner):
        return pltpu.make_async_remote_copy(
            src_ref=src, dst_ref=mbuf.at[owner], send_sem=met_send.at[way, step],
            recv_sem=met_recv.at[way, step], device_id=(target(way), col), device_id_type=MESH,
        )

    def fit_copy(way, atom, step, src, owner):
        return pltpu.make_async_remote_copy(
            src_ref=src, dst_ref=gat.at[owner, atom], send_sem=fit_send.at[way, atom, step],
            recv_sem=fit_recv.at[way, atom, step], device_id=(target(way), col), device_id_type=MESH,
        )

    def note_copy(k):
        return pltpu.make_async_remote_copy(
            src_ref=note, dst_ref=notes.at[row], send_sem=note_send.at[k],
            recv_sem=note_recv.at[k], device_id=(lax.rem(row + k, n), col), device_id_type=MESH,
        )

    def reach(way, atom):
        return hops[(way + atom) % 2]

    for way in range(2):
        if hops[way] > 0:
            met_copy(way, 0, metric, row).start()
    for k in range(1, n):
        note_copy(k).start()
    for atom in range(atoms):
        for way in range(2):
            if reach(way, atom) > 0:
                fit_copy(way, atom, 0, fit.at[atom], row).start()

    for step in range(1, half + 1):
        for way in range(2):
            if step <= hops[way]:
                owner = source(way, step)
                met_copy(way, step - 1, mbuf.at[owner], owner).wait_recv()
                if step < hops[way]:
                    met_copy(way, step, mbuf.at[owner], owner).start()
    for k in range(1, n):
        note_copy(k).wait_recv()
    to_table = pltpu.make_async_copy(notes, table, table_sem)
    to_table.start()
    for q in range(blocks):
        mfull[q] = mbuf[:, q].reshape(aux, aux).astype(jnp.bfloat16)
    to_table.wait()

    def fitted(tile, owner, atom, s):
        return jnp.dot(
            tile, mfull[table[owner, atom, s]], preferred_element_type=jnp.float32
        ).astype(jnp.bfloat16)

    def send_part(a):
        dest = a // share
        return pltpu.make_async_remote_copy(
            src_ref=part.at[a], dst_ref=red.at[col, lax.rem(a, share)], send_sem=red_send.at[a],
            recv_sem=red_recv.at[col, lax.rem(a, share)], device_id=(row, dest), device_id_type=MESH,
        )

    def combine(left, owner, atom):
        count = table[owner, atom, slots]
        right = [
            wide[jnp.where(s < count, table[owner, atom, s], blocks)] for s in range(slots)
        ]
        a = owner * atoms + atom
        part[a] = jnp.dot(
            jnp.concatenate(left, axis=1), jnp.concatenate(right, axis=0),
            preferred_element_type=jnp.float32,
        )

        @pl.when(a // share != col)
        def _():
            send_part(a).start()

    def process(view, owner, atom):
        combine([fitted(view[s], owner, atom, s) for s in range(slots)], owner, atom)

    own = []
    for atom in range(atoms):
        own.append([fitted(fit[atom, s], row, atom, s) for s in range(slots)])
        for s in range(slots):
            turned[atom, s] = own[atom][s].T
        turned[atom, slots] = jnp.zeros((aux, rows), jnp.bfloat16)
    for q in range(blocks):
        for atom in range(atoms):
            where = jnp.int32(slots)
            for s in range(slots):
                hit = (table[row, atom, s] == q) & (s < table[row, atom, slots])
                where = jnp.where(hit, s, where)
            wide[q, :, atom * rows : (atom + 1) * rows] = turned[atom, where]
    wide[blocks] = jnp.zeros_like(wide[blocks])
    for atom in range(atoms):
        combine(own[atom], row, atom)

    def arrive(step, pairs):
        for way, atom, last in pairs:
            owner = source(way, step)
            fit_copy(way, atom, step - 1, gat.at[owner, atom], owner).wait_recv()
            if not last:
                fit_copy(way, atom, step, gat.at[owner, atom], owner).start()
        for way, atom, _ in pairs:
            owner = source(way, step)
            process(gat.at[owner, atom], owner, atom)

    every = [(way, atom) for atom in range(atoms) for way in range(2)]
    for step in range(1, half + 1):
        arrive(step, [(w, b, step == reach(w, b)) for w, b in every if step <= reach(w, b)])

    for j in range(share):
        total = part[col * share + j]
        for k in range(1, m):
            peer = lax.rem(col + k, m)
            pltpu.make_async_remote_copy(
                src_ref=part.at[0], dst_ref=red.at[peer, j], send_sem=red_send.at[0],
                recv_sem=red_recv.at[peer, j], device_id=(row, peer), device_id_type=MESH,
            ).wait_recv()
            total += red[peer, j]
        out[j * rows : (j + 1) * rows, :] = total

    for way in range(2):
        for step in range(hops[way]):
            met_copy(way, step, metric, row).wait_send()
        for atom in range(atoms):
            for step in range(reach(way, atom)):
                fit_copy(way, atom, step, fit.at[atom], row).wait_send()
    for k in range(1, n):
        note_copy(k).wait_send()

    @pl.loop(0, n * atoms)
    def _(a):
        @pl.when(a // share != col)
        def _():
            send_part(a).wait_send()


def local(n, m, fit, aux_list, aux_count, metric):
    atoms, slots, rows, aux = fit.shape
    blocks, depth, _ = metric.shape
    share = n * atoms // m
    if depth % 16:
        metric = metric.astype(jnp.float32)
    dma = pltpu.SemaphoreType.DMA
    vmem = pl.BlockSpec(memory_space=pltpu.VMEM)
    summed = pl.pallas_call(
        functools.partial(kernel, n, m, share),
        out_shape=jax.ShapeDtypeStruct((share * rows, atoms * rows), jnp.float32),
        in_specs=[vmem] * 4,
        out_specs=vmem,
        scratch_shapes=[
            pltpu.VMEM((n, blocks, depth, aux), metric.dtype),
            pltpu.VMEM((blocks, aux, aux), jnp.bfloat16),
            pltpu.VMEM((n, atoms, slots, rows, aux), jnp.bfloat16),
            pltpu.VMEM((8, 128), jnp.int32),
            pltpu.VMEM((n, 8, 128), jnp.int32),
            pltpu.SMEM((n, 8, 128), jnp.int32),
            pltpu.VMEM((atoms, slots + 1, aux, rows), jnp.bfloat16),
            pltpu.VMEM((blocks + 1, aux, atoms * rows), jnp.bfloat16),
            pltpu.VMEM((n * atoms, rows, atoms * rows), jnp.float32),
            pltpu.VMEM((m, share, rows, atoms * rows), jnp.float32),
            dma((2, n)),
            dma((2, n)),
            dma((2, atoms, n)),
            dma((2, atoms, n)),
            dma((n,)),
            dma((n,)),
            dma,
            dma((n * atoms,)),
            dma((m, share)),
        ],
        compiler_params=pltpu.CompilerParams(
            collective_id=0, has_side_effects=True, vmem_limit_bytes=48 * 1024 * 1024
        ),
        cost_estimate=pl.CostEstimate(
            flops=2 * n * atoms * slots * rows * aux * (aux + atoms * rows),
            bytes_accessed=2 * n * atoms * slots * rows * aux,
            transcendentals=0,
        ),
    )(fit, metric, aux_list, aux_count)
    return summed * (1.0 / (slots * m * aux) ** 0.5)


def solution(mesh):
    placed = (P("row", "col", None, None), P("row", "col"), P("row", "col"), P("col", "row", None))
    return jax.shard_map(
        functools.partial(local, mesh.shape["row"], mesh.shape["col"]),
        mesh=mesh, in_specs=placed, out_specs=P("col", "row"), check_vma=False,
    )
```

```python
import functools

import jax
import jax.numpy as jnp
from jax import lax
from jax.experimental import pallas as pl
from jax.experimental.pallas import tpu as pltpu
from jax.sharding import PartitionSpec as P

MESH = pl.DeviceIdType.MESH


def kernel(
    n, m, share, fit, metric, lst, cnt, out,
    mbuf, mfull, gat, note, notes, table, turned, wide, part, red,
    keep_sem, met_send, met_recv, fit_send, fit_recv, note_send, note_recv, table_sem, red_send, red_recv,
):
    atoms, slots, rows, aux = fit.shape
    blocks = metric.shape[0]
    cuts = 3 if slots % 3 == 0 else 1
    span = slots // cuts
    pieces = atoms * cuts
    half = n // 2
    hops = (half, n - 1 - half)
    row = lax.axis_index("row")
    col = lax.axis_index("col")

    def at_position(p):
        p = lax.rem(p + n, n)
        return jnp.where(p < (n + 1) // 2, 2 * p, 2 * (n - 1 - p) + 1)

    place = jnp.where(lax.rem(row, 2) == 0, row // 2, n - 1 - row // 2)

    def source(way, step):
        return at_position(place - step if way == 0 else place + step)

    def target(way):
        return at_position(place + 1 if way == 0 else place + n - 1)

    barrier = pltpu.get_barrier_semaphore()
    for k in range(1, n):
        pl.semaphore_signal(barrier, inc=1, device_id=(lax.rem(row + k, n), col), device_id_type=MESH)
    for k in range(1, m):
        pl.semaphore_signal(barrier, inc=1, device_id=(row, lax.rem(col + k, m)), device_id_type=MESH)
    note[...] = jnp.zeros_like(note)
    note[0:atoms, 0:slots] = lst[...]
    note[atoms : atoms + 1, 0:atoms] = cnt[...]
    notes[row] = note[...]
    keep_fit = pltpu.make_async_copy(fit, gat.at[row], keep_sem.at[0])
    keep_fit.start()
    keep_metric = pltpu.make_async_copy(metric, mbuf.at[row], keep_sem.at[1])
    keep_metric.start()
    pl.semaphore_wait(barrier, n + m - 2)

    def met_copy(way, step, src, owner):
        return pltpu.make_async_remote_copy(
            src_ref=src, dst_ref=mbuf.at[owner], send_sem=met_send.at[way, step],
            recv_sem=met_recv.at[way, step], device_id=(target(way), col), device_id_type=MESH,
        )

    def piece(ref, u):
        return ref.at[u // cuts, pl.ds((u % cuts) * span, span)]

    def fit_copy(way, u, step, owner):
        src = fit if step == 0 else gat.at[owner]
        return pltpu.make_async_remote_copy(
            src_ref=piece(src, u), dst_ref=piece(gat.at[owner], u), send_sem=fit_send.at[way, u, step],
            recv_sem=fit_recv.at[way, u, step], device_id=(target(way), col), device_id_type=MESH,
        )

    def note_copy(k):
        return pltpu.make_async_remote_copy(
            src_ref=note, dst_ref=notes.at[row], send_sem=note_send.at[k],
            recv_sem=note_recv.at[k], device_id=(lax.rem(row + k, n), col), device_id_type=MESH,
        )

    def reach(way, u):
        return hops[(way + u) % 2]

    def send_own(u):
        for way in range(2):
            if reach(way, u) > 0:
                fit_copy(way, u, 0, row).start()

    def arrive(way, u, step):
        owner = source(way, step)
        fit_copy(way, u, step - 1, owner).wait_recv()
        if step < reach(way, u):
            fit_copy(way, u, step, owner).start()

    for way in range(2):
        if hops[way] > 0:
            met_copy(way, 0, metric, row).start()
    send_own(0)
    for k in range(1, n):
        note_copy(k).start()
    for step in range(1, half + 1):
        for way in range(2):
            if step <= hops[way]:
                owner = source(way, step)
                met_copy(way, step - 1, mbuf.at[owner], owner).wait_recv()
                if step < hops[way]:
                    met_copy(way, step, mbuf.at[owner], owner).start()
        if step < pieces:
            send_own(step)
    for u in range(half + 1, pieces):
        send_own(u)
    for k in range(1, n):
        note_copy(k).wait_recv()
    to_table = pltpu.make_async_copy(notes, table, table_sem)
    to_table.start()
    keep_fit.wait()
    keep_metric.wait()
    for u in range(pieces):
        for way in range(2):
            if reach(way, u) > 0:
                arrive(way, u, 1)
    for q in range(blocks):
        mfull[q] = mbuf[:, q].reshape(aux, aux).astype(jnp.bfloat16)
    to_table.wait()

    def fitted(tile, owner, atom, s):
        return jnp.dot(
            tile, mfull[table[owner, atom, s]], preferred_element_type=jnp.float32
        ).astype(jnp.bfloat16)

    def send_part(a):
        dest = a // share
        return pltpu.make_async_remote_copy(
            src_ref=part.at[a], dst_ref=red.at[col, lax.rem(a, share)], send_sem=red_send.at[a],
            recv_sem=red_recv.at[col, lax.rem(a, share)], device_id=(row, dest), device_id_type=MESH,
        )

    def combine(left, owner, atom):
        count = table[owner, atoms, atom]
        right = [
            wide[jnp.where(s < count, table[owner, atom, s], blocks)] for s in range(slots)
        ]
        a = owner * atoms + atom
        part[a] = jnp.dot(
            jnp.concatenate(left, axis=1), jnp.concatenate(right, axis=0),
            preferred_element_type=jnp.float32,
        )

        @pl.when(a // share != col)
        def _():
            send_part(a).start()

    def process(owner, atom):
        combine([fitted(gat[owner, atom, s], owner, atom, s) for s in range(slots)], owner, atom)

    own = []
    for atom in range(atoms):
        own.append([fitted(gat[row, atom, s], row, atom, s) for s in range(slots)])
        for s in range(slots):
            turned[atom, s] = own[atom][s].T
        turned[atom, slots] = jnp.zeros((aux, rows), jnp.bfloat16)
    for q in range(blocks):
        for atom in range(atoms):
            where = jnp.int32(slots)
            for s in range(slots):
                hit = (table[row, atom, s] == q) & (s < table[row, atoms, atom])
                where = jnp.where(hit, s, where)
            wide[q, :, atom * rows : (atom + 1) * rows] = turned[atom, where]
    wide[blocks] = jnp.zeros_like(wide[blocks])
    for atom in range(atoms):
        combine(own[atom], row, atom)

    for step in range(1, half + 1):
        both = step <= min(hops)
        for atom in range(atoms):
            for u in range(atom * cuts, (atom + 1) * cuts):
                for way in range(2):
                    if 1 < step <= reach(way, u):
                        arrive(way, u, step)
            process(source(0, step), atom)
            if both:
                process(source(1, step), atom)

    for j in range(share):
        total = part[col * share + j]
        for k in range(1, m):
            peer = lax.rem(col + k, m)
            pltpu.make_async_remote_copy(
                src_ref=part.at[0], dst_ref=red.at[peer, j], send_sem=red_send.at[0],
                recv_sem=red_recv.at[peer, j], device_id=(row, peer), device_id_type=MESH,
            ).wait_recv()
            total += red[peer, j]
        out[j * rows : (j + 1) * rows, :] = total

    for way in range(2):
        for step in range(hops[way]):
            met_copy(way, step, metric, row).wait_send()
        for u in range(pieces):
            for step in range(reach(way, u)):
                fit_copy(way, u, step, row).wait_send()
    for k in range(1, n):
        note_copy(k).wait_send()

    @pl.loop(0, n * atoms)
    def _(a):
        @pl.when(a // share != col)
        def _():
            send_part(a).wait_send()


def local(n, m, fit, aux_list, aux_count, metric):
    atoms, slots, rows, aux = fit.shape
    blocks, depth, _ = metric.shape
    share = n * atoms // m
    if depth % 16:
        metric = metric.astype(jnp.float32)
    dma = pltpu.SemaphoreType.DMA
    vmem = pl.BlockSpec(memory_space=pltpu.VMEM)
    summed = pl.pallas_call(
        functools.partial(kernel, n, m, share),
        out_shape=jax.ShapeDtypeStruct((share * rows, atoms * rows), jnp.float32),
        in_specs=[pl.BlockSpec(memory_space=pltpu.HBM)] * 2 + [vmem] * 2,
        out_specs=vmem,
        scratch_shapes=[
            pltpu.VMEM((n, blocks, depth, aux), metric.dtype),
            pltpu.VMEM((blocks, aux, aux), jnp.bfloat16),
            pltpu.VMEM((n, atoms, slots, rows, aux), jnp.bfloat16),
            pltpu.VMEM((8, 128), jnp.int32),
            pltpu.VMEM((n, 8, 128), jnp.int32),
            pltpu.SMEM((n, 8, 128), jnp.int32),
            pltpu.VMEM((atoms, slots + 1, aux, rows), jnp.bfloat16),
            pltpu.VMEM((blocks + 1, aux, atoms * rows), jnp.bfloat16),
            pltpu.VMEM((n * atoms, rows, atoms * rows), jnp.float32),
            pltpu.VMEM((m, share, rows, atoms * rows), jnp.float32),
            dma((2,)),
            dma((2, n)),
            dma((2, n)),
            dma((2, atoms * slots, n)),
            dma((2, atoms * slots, n)),
            dma((n,)),
            dma((n,)),
            dma,
            dma((n * atoms,)),
            dma((m, share)),
        ],
        compiler_params=pltpu.CompilerParams(
            collective_id=0, has_side_effects=True, vmem_limit_bytes=48 * 1024 * 1024
        ),
        cost_estimate=pl.CostEstimate(
            flops=2 * n * atoms * slots * rows * aux * (aux + atoms * rows),
            bytes_accessed=2 * n * atoms * slots * rows * aux,
            transcendentals=0,
        ),
    )(fit, metric, aux_list, aux_count.T)
    return summed * (1.0 / (slots * m * aux) ** 0.5)


def solution(mesh):
    placed = (P("row", "col", None, None), P("row", "col"), P("row", "col"), P("col", "row", None))
    return jax.shard_map(
        functools.partial(local, mesh.shape["row"], mesh.shape["col"]),
        mesh=mesh, in_specs=placed, out_specs=P("col", "row"), check_vma=False,
    )
```

```python
import functools

import jax
import jax.numpy as jnp
from jax import lax
from jax.experimental import pallas as pl
from jax.experimental.pallas import tpu as pltpu
from jax.sharding import PartitionSpec as P

MESH = pl.DeviceIdType.MESH


def kernel(
    n, m, share, fit, metric, lst, cnt, out,
    mbuf, mfull, gat, note, notes, table, turned, wide, part, mid, red,
    keep_sem, met_send, met_recv, fit_send, fit_recv, note_send, note_recv, table_sem, mid_recv, red_send, red_recv,
):
    atoms, slots, rows, aux = fit.shape
    blocks = metric.shape[0]
    cuts = 4
    span = rows // cuts
    pieces = atoms * cuts
    feed = 2
    half = n // 2
    hops = (half, n - 1 - half)
    row = lax.axis_index("row")
    col = lax.axis_index("col")

    def at_position(p):
        p = lax.rem(p + n, n)
        return jnp.where(p < (n + 1) // 2, 2 * p, 2 * (n - 1 - p) + 1)

    place = jnp.where(lax.rem(row, 2) == 0, row // 2, n - 1 - row // 2)

    def source(way, step):
        return at_position(place - step if way == 0 else place + step)

    def target(way):
        return at_position(place + 1 if way == 0 else place + n - 1)

    barrier = pltpu.get_barrier_semaphore()
    for k in range(1, n):
        pl.semaphore_signal(barrier, inc=1, device_id=(lax.rem(row + k, n), col), device_id_type=MESH)
    for k in range(1, m):
        pl.semaphore_signal(barrier, inc=1, device_id=(row, lax.rem(col + k, m)), device_id_type=MESH)
    note[...] = jnp.zeros_like(note)
    note[0:atoms, 0:slots] = lst[...]
    note[atoms : atoms + 1, 0:atoms] = cnt[...]
    notes[row] = note[...]
    keep_fit = pltpu.make_async_copy(fit, gat.at[row], keep_sem.at[0])
    keep_fit.start()
    keep_metric = pltpu.make_async_copy(metric, mbuf.at[row], keep_sem.at[1])
    keep_metric.start()
    pl.semaphore_wait(barrier, n + m - 2)

    def met_copy(way, step, src, owner):
        return pltpu.make_async_remote_copy(
            src_ref=src, dst_ref=mbuf.at[owner], send_sem=met_send.at[way, step],
            recv_sem=met_recv.at[way, step], device_id=(target(way), col), device_id_type=MESH,
        )

    def piece(ref, u):
        return ref.at[u // cuts, :, pl.ds((u % cuts) * span, span)]

    def fit_copy(way, u, step, owner):
        src = fit if step == 0 else gat.at[owner]
        return pltpu.make_async_remote_copy(
            src_ref=piece(src, u), dst_ref=piece(gat.at[owner], u), send_sem=fit_send.at[way, u, step],
            recv_sem=fit_recv.at[way, u, step], device_id=(target(way), col), device_id_type=MESH,
        )

    def note_copy(k):
        return pltpu.make_async_remote_copy(
            src_ref=note, dst_ref=notes.at[row], send_sem=note_send.at[k],
            recv_sem=note_recv.at[k], device_id=(lax.rem(row + k, n), col), device_id_type=MESH,
        )

    def reach(way, u):
        return hops[(way + u) % 2]

    def send_own(u):
        for way in range(2):
            if reach(way, u) > 0:
                fit_copy(way, u, 0, row).start()

    def arrive(way, u, step):
        owner = source(way, step)
        fit_copy(way, u, step - 1, owner).wait_recv()
        if step < reach(way, u):
            fit_copy(way, u, step, owner).start()

    for way in range(2):
        if hops[way] > 0:
            met_copy(way, 0, metric, row).start()
    for u in range(min(feed, pieces)):
        send_own(u)
    for k in range(1, n):
        note_copy(k).start()
    for step in range(1, half + 1):
        for way in range(2):
            if step <= hops[way]:
                owner = source(way, step)
                met_copy(way, step - 1, mbuf.at[owner], owner).wait_recv()
                if step < hops[way]:
                    met_copy(way, step, mbuf.at[owner], owner).start()
        for u in range(step * feed, min(pieces, (step + 1) * feed)):
            send_own(u)
    for u in range((half + 1) * feed, pieces):
        send_own(u)
    for k in range(1, n):
        note_copy(k).wait_recv()
    to_table = pltpu.make_async_copy(notes, table, table_sem)
    to_table.start()
    keep_fit.wait()
    keep_metric.wait()
    for u in range(pieces):
        for way in range(2):
            if reach(way, u) > 0:
                arrive(way, u, 1)
    for q in range(blocks):
        mfull[q] = mbuf[:, q].reshape(aux, aux).astype(jnp.bfloat16)
    to_table.wait()

    def fitted(tile, owner, atom, s):
        return jnp.dot(
            tile, mfull[table[owner, atom, s]], preferred_element_type=jnp.float32
        ).astype(jnp.bfloat16)

    twin = col + 1 - 2 * lax.rem(col, 2)

    def send_part(a, low, size):
        lines = pl.ds(low, size)
        return pltpu.make_async_remote_copy(
            src_ref=part.at[a, lines], dst_ref=red.at[col, lax.rem(a, share), lines], send_sem=red_send.at[a],
            recv_sem=red_recv.at[col, lax.rem(a, share)], device_id=(row, a // share), device_id_type=MESH,
        )

    def send_twin(a, low, size):
        lines = pl.ds(low, size)
        return pltpu.make_async_remote_copy(
            src_ref=part.at[a, lines], dst_ref=mid.at[a, lines], send_sem=red_send.at[a],
            recv_sem=mid_recv.at[a, low // span], device_id=(row, twin), device_id_type=MESH,
        )

    def far(a):
        return (a // share) // 2 != col // 2

    def same(a):
        return lax.rem(a // share, 2) == lax.rem(col, 2)

    waiting = []

    def pass_on():
        a, low, size = waiting.pop(0)

        @pl.when(far(a) & same(a))
        def _():
            send_twin(a, low, size).wait_recv()
            part[a, low : low + size] += mid[a, low : low + size]
            send_part(a, low, size).start()

    def combine(left, owner, atom, low=0, size=rows):
        count = table[owner, atoms, atom]
        right = [
            wide[jnp.where(s < count, table[owner, atom, s], blocks)] for s in range(slots)
        ]
        a = owner * atoms + atom
        part[a, low : low + size] = jnp.dot(
            jnp.concatenate(left, axis=1), jnp.concatenate(right, axis=0),
            preferred_element_type=jnp.float32,
        )

        @pl.when(far(a) & jnp.logical_not(same(a)))
        def _():
            send_twin(a, low, size).start()

        @pl.when(a // share == twin)
        def _():
            send_part(a, low, size).start()

        waiting.append((a, low, size))
        if len(waiting) > 2:
            pass_on()

    def process(owner, atom, low=0, size=rows):
        left = [
            fitted(gat[owner, atom, s, low : low + size, :], owner, atom, s) for s in range(slots)
        ]
        combine(left, owner, atom, low, size)

    own = []
    for atom in range(atoms):
        own.append([fitted(gat[row, atom, s], row, atom, s) for s in range(slots)])
        for s in range(slots):
            turned[atom, s] = own[atom][s].T
        turned[atom, slots] = jnp.zeros((aux, rows), jnp.bfloat16)
    for q in range(blocks):
        for atom in range(atoms):
            where = jnp.int32(slots)
            for s in range(slots):
                hit = (table[row, atom, s] == q) & (s < table[row, atoms, atom])
                where = jnp.where(hit, s, where)
            wide[q, :, atom * rows : (atom + 1) * rows] = turned[atom, where]
    wide[blocks] = jnp.zeros_like(wide[blocks])
    for atom in range(atoms):
        combine(own[atom], row, atom)

    for step in range(1, min(hops) + 1):
        for atom in range(atoms):
            for u in range(atom * cuts, (atom + 1) * cuts):
                for way in range(2):
                    if step > 1:
                        arrive(way, u, step)
            for way in range(2):
                process(source(way, step), atom)
    if hops[0] > hops[1]:
        for u in range(pieces):
            if half > 1:
                arrive(u % 2, u, half)
            process(source(0, half), u // cuts, (u % cuts) * span, span)

    while waiting:
        pass_on()
    for j in range(share):
        total = part[col * share + j]
        for peer in [twin] + [lax.rem(col + k, m) for k in range(2, m, 2)]:
            pltpu.make_async_remote_copy(
                src_ref=part.at[0], dst_ref=red.at[peer, j], send_sem=red_send.at[0],
                recv_sem=red_recv.at[peer, j], device_id=(row, peer), device_id_type=MESH,
            ).wait_recv()
            total += red[peer, j]
        out[j * rows : (j + 1) * rows, :] = total

    for way in range(2):
        for step in range(hops[way]):
            met_copy(way, step, metric, row).wait_send()
        for u in range(pieces):
            for step in range(reach(way, u)):
                fit_copy(way, u, step, row).wait_send()
    for k in range(1, n):
        note_copy(k).wait_send()

    @pl.loop(0, n * atoms)
    def _(a):
        @pl.when(a // share != col)
        def _():
            send_part(a, 0, rows).wait_send()


def local(n, m, fit, aux_list, aux_count, metric):
    atoms, slots, rows, aux = fit.shape
    blocks, depth, _ = metric.shape
    share = n * atoms // m
    if depth % 16:
        metric = metric.astype(jnp.float32)
    dma = pltpu.SemaphoreType.DMA
    vmem = pl.BlockSpec(memory_space=pltpu.VMEM)
    summed = pl.pallas_call(
        functools.partial(kernel, n, m, share),
        out_shape=jax.ShapeDtypeStruct((share * rows, atoms * rows), jnp.float32),
        in_specs=[pl.BlockSpec(memory_space=pltpu.HBM)] * 2 + [vmem] * 2,
        out_specs=vmem,
        scratch_shapes=[
            pltpu.VMEM((n, blocks, depth, aux), metric.dtype),
            pltpu.VMEM((blocks, aux, aux), jnp.bfloat16),
            pltpu.VMEM((n, atoms, slots, rows, aux), jnp.bfloat16),
            pltpu.VMEM((8, 128), jnp.int32),
            pltpu.VMEM((n, 8, 128), jnp.int32),
            pltpu.SMEM((n, 8, 128), jnp.int32),
            pltpu.VMEM((atoms, slots + 1, aux, rows), jnp.bfloat16),
            pltpu.VMEM((blocks + 1, aux, atoms * rows), jnp.bfloat16),
            pltpu.VMEM((n * atoms, rows, atoms * rows), jnp.float32),
            pltpu.VMEM((n * atoms, rows, atoms * rows), jnp.float32),
            pltpu.VMEM((m, share, rows, atoms * rows), jnp.float32),
            dma((2,)),
            dma((2, n)),
            dma((2, n)),
            dma((2, 4 * atoms, n)),
            dma((2, 4 * atoms, n)),
            dma((n,)),
            dma((n,)),
            dma,
            dma((n * atoms, 4)),
            dma((n * atoms,)),
            dma((m, share)),
        ],
        compiler_params=pltpu.CompilerParams(
            collective_id=0, has_side_effects=True, vmem_limit_bytes=48 * 1024 * 1024
        ),
        cost_estimate=pl.CostEstimate(
            flops=2 * n * atoms * slots * rows * aux * (aux + atoms * rows),
            bytes_accessed=2 * n * atoms * slots * rows * aux,
            transcendentals=0,
        ),
    )(fit, metric, aux_list, aux_count.T)
    return summed * (1.0 / (slots * m * aux) ** 0.5)


def solution(mesh):
    placed = (P("row", "col", None, None), P("row", "col"), P("row", "col"), P("col", "row", None))
    return jax.shard_map(
        functools.partial(local, mesh.shape["row"], mesh.shape["col"]),
        mesh=mesh, in_specs=placed, out_specs=P("col", "row"), check_vma=False,
    )
```
